32 devices in a mesh: member: 4 (over x, core), lat: 4 (over z), lon: 2 (over y).
Axes of the slice: x: 2, y: 2, z: 4, core: 2. Of those that a mesh axis runs over, the one named last changes fastest.
Arguments:
- analysis: bfloat16 [96, 16, 256], P('lat', 'lon', 'member'), may hold values from -6 to 6
- noise: bfloat16 [4, 96, 16, 256], P('member', 'lat', 'lon'), may hold values from -6 to 6
- w_in: bfloat16 [256, 256], replicated, may hold values from -0.375 to 0.375
- lat_offsets: int32 [96, 9], P('lat'), may hold values from -1 to 1, as said below
- lon_offsets: int32 [96, 9], P('lat'), may hold values from -8 to 8, as said below
- psi: float32 [96, 9, 3], P('lat'), may hold values from -2 to 2
- w_disco: bfloat16 [3, 256, 256], replicated, may hold values from -0.21875 to 0.21875
- norm_gain: float32 [256], replicated, may hold values from 0.1 to 1.9
- w_up: bfloat16 [256, 512], replicated, may hold values from -0.375 to 0.375
- bias_up: float32 [512], replicated, may hold values from -4 to 4
- w_down: bfloat16 [512, 256], replicated, may hold values from -0.25 to 0.25
Outputs:
- states: bfloat16 [4, 96, 16, 256], P('member', 'lat', 'lon')
The draws below stay inside these ranges and needn't reach their ends.
Inputs may be any that keep to these rules, and one draw needn't show every extreme that they name: `lat_offsets`: columns 0 and 1 of every row are -1 and +1; the others lie in -1 to 1. `lon_offsets`: at row i with r = min(i, 95 - i), every offset has magnitude at most s = max(1, 8 - (8 * r) // max(24, 1)), and column 2 equals s or -s; row 0 holds 8 and row 95 holds -8.
All inputs are finite; a program needn't handle non-finite values.
Results may differ from the reference program's by a relative error of at most 0.02.
Values may be sent and summed in bfloat16 or wider, within the bound.
No kernel may reach another device: no remote copies, remote signals or barrier semaphores. Data moves between devices by JAX's collectives and lax.ppermute only.
A program may use at most 64 MiB of HBM per device.

```python
import jax
import jax.numpy as jnp
from jax import lax

C = 256
HID = 512
K = 9
B = 3
HW = 8
PASSES = 2
MEMBERS = 4
NLAT = 96
NLON = 16


def draw_lat_offsets(key, part):
    key = jax.random.fold_in(key, 11)
    values = jax.random.randint(key, (NLAT, K), -1, 2)
    values = values.at[:, 0].set(-1).at[:, 1].set(1)
    return values.astype(jnp.int32)


def draw_lon_offsets(key, part):
    key = jax.random.fold_in(key, 23)
    first_key, second_key = jax.random.split(key)
    rows = jnp.arange(NLAT, dtype=jnp.int32)
    distance = jnp.minimum(rows, NLAT - 1 - rows)
    span = jnp.maximum(1, HW - HW * distance // max(NLAT // 4, 1))
    raw_values = jax.random.randint(first_key, (NLAT, K), 0, 2 * HW + 1)
    values = raw_values % (2 * span[:, None] + 1) - span[:, None]
    signs = 2 * jax.random.randint(second_key, (NLAT,), 0, 2) - 1
    signs = signs.at[0].set(1).at[NLAT - 1].set(-1)
    values = values.at[:, 2].set(signs * span)
    return values.astype(jnp.int32)


def shard_levels(own_key, dims, pieces, smallest, high):
    loudness, own = 1.0, jax.random.fold_in(own_key, 6)
    for dim, parts in pieces:
        heights = jnp.exp(jax.random.uniform(jax.random.fold_in(own, dim), (parts,), jnp.float32, smallest / len(pieces), high / len(pieces)))
        loudness = loudness * jnp.repeat(heights, dims[dim] // parts).reshape([-1 if axis == dim else 1 for axis in range(len(dims))])
    return loudness


def bell_draw(stream_key, extent, scale, bound, shards=(), kind=jnp.bfloat16):
    values = jax.random.normal(stream_key, extent, jnp.float32) * scale
    if len(shards) > 0:
        values = shard_levels(stream_key, extent, shards, -0.22, 0.18) * values
    return jnp.clip(values, min=-bound, max=bound).astype(kind)


def setup_inputs(seed: int = 0) -> dict:
    arg_keys = jax.random.split(jax.random.key(seed), 12)
    return {
        "analysis": bell_draw(arg_keys[0], (NLAT, NLON, C), 1.0, 6.0, ((0, 4), (1, 2), (2, 4))),
        "noise": bell_draw(arg_keys[1], (MEMBERS, NLAT, NLON, C), 1.0, 6.0, ((0, 4), (1, 4), (2, 2))),
        "w_in": bell_draw(arg_keys[2], (C, C), C ** -0.5, 0.375),
        "lat_offsets": draw_lat_offsets(jax.random.fold_in(arg_keys[11], 71), 0),
        "lon_offsets": draw_lon_offsets(jax.random.fold_in(arg_keys[11], 71), 0),
        "psi": bell_draw(arg_keys[5], (NLAT, K, B), K ** -0.5, 2.0, ((0, 4),), jnp.float32),
        "w_disco": bell_draw(arg_keys[6], (B, C, C), (B * C) ** -0.5, 0.21875),
        "norm_gain": jnp.clip(1.0 + 0.18 * jax.random.normal(arg_keys[7], (C,), jnp.float32), 0.1, 1.9),
        "w_up": bell_draw(arg_keys[8], (C, HID), C ** -0.5, 0.375),
        "bias_up": bell_draw(arg_keys[9], (HID,), 1.0, 4.0, (), jnp.float32),
        "w_down": bell_draw(arg_keys[10], (HID, C), HID ** -0.5, 0.25),
    }


def one_pass(state, lat_offsets, lon_offsets, psi, w_disco, norm_gain, w_up, bias_up, w_down):
    half = NLON // 2
    top = jnp.roll(state[:1], half, axis=1)
    bottom = jnp.roll(state[-1:], half, axis=1)
    extended = jnp.concatenate([top, state, bottom], axis=0)
    row_ids = jnp.arange(NLAT, dtype=jnp.int32)
    col_ids = jnp.arange(NLON, dtype=jnp.int32)
    mix = jnp.zeros((B, NLAT, NLON, C), jnp.float32)
    for point in range(K):
        picked = jnp.take(extended, row_ids + lat_offsets[:, point] + 1, axis=0)
        columns = (col_ids[None, :] + lon_offsets[:, point][:, None]) % NLON
        columns = jnp.broadcast_to(columns[:, :, None], (NLAT, NLON, C))
        moved = jnp.take_along_axis(picked, columns, axis=1).astype(jnp.float32)
        mix = mix + psi[:, point, :].T[:, :, None, None] * moved[None]
    mix = mix.astype(jnp.bfloat16)
    inner = state.astype(jnp.float32).reshape(-1, C)
    for basis in range(B):
        inner = inner + jnp.dot(mix[basis].reshape(-1, C), w_disco[basis], preferred_element_type=jnp.float32)
    mean = lax.optimization_barrier(jnp.mean(inner, axis=1, keepdims=True))
    centred = inner - mean
    variance = lax.optimization_barrier(jnp.mean(centred * centred, axis=1, keepdims=True))
    normed = (centred * lax.rsqrt(variance + 1e-05) * norm_gain).astype(jnp.bfloat16)
    hidden = jax.nn.gelu(jnp.dot(normed, w_up, preferred_element_type=jnp.float32) + bias_up).astype(jnp.bfloat16)
    result = inner + jnp.dot(hidden, w_down, preferred_element_type=jnp.float32)
    return result.astype(jnp.bfloat16).reshape(NLAT, NLON, C)

def reference(analysis, noise, w_in, lat_offsets, lon_offsets, psi, w_disco, norm_gain, w_up, bias_up, w_down):
    base = jnp.dot(analysis.reshape(-1, C), w_in, preferred_element_type=jnp.float32)

    def member_run(member_noise):
        state = (base + member_noise.reshape(-1, C).astype(jnp.float32)).astype(jnp.bfloat16).reshape(NLAT, NLON, C)
        for step in range(PASSES):
            state = one_pass(state, lat_offsets, lon_offsets, psi, w_disco, norm_gain, w_up, bias_up, w_down)
        return state
    return lax.map(member_run, noise)
```

```python
import functools

import jax
import jax.numpy as jnp
from jax import lax
from jax.experimental import pallas as pl
from jax.experimental.pallas import tpu as pltpu
from jax.sharding import PartitionSpec as P

B = 3
HW = 8
PASSES = 2
K = 9
GROUP = 6


def ring_padded(cells, sides, width, closed):
    for axis, dim in sides:
        count = lax.axis_size(axis)
        ends = count if closed else count - 1
        head = lax.slice_in_dim(cells, 0, width, axis=dim)
        tail = lax.slice_in_dim(cells, cells.shape[dim] - width, cells.shape[dim], axis=dim)
        cells = jnp.concatenate(
            [
                lax.ppermute(tail, axis, [(i, (i + 1) % count) for i in range(ends)]),
                cells,
                lax.ppermute(head, axis, [((i + 1) % count, i) for i in range(ends)]),
            ],
            axis=dim,
        )
    return cells


def extend(state):
    count = lax.axis_size("lon")
    rows = ring_padded(state, (("lat", 0),), 1, False)
    edges = jnp.stack([state[0], state[-1]])
    flipped = lax.ppermute(edges, "lon", [(i, (i + count // 2) % count) for i in range(count)])
    band = lax.axis_index("lat")
    last_band = lax.axis_size("lat") - 1
    top = jnp.where(band == 0, flipped[0], rows[0])
    bottom = jnp.where(band == last_band, flipped[1], rows[-1])
    rows = jnp.concatenate([top[None], rows[1:-1], bottom[None]], axis=0)
    return ring_padded(rows, (("lon", 1),), HW, True)


def window_pass(state, lat_offsets, lon_offsets, psi, w_disco, norm_gain, w_up, bias_up, w_down):
    row_count, col_count, width = state.shape
    extended = extend(state)
    span = col_count + 2 * HW
    stacked = jnp.concatenate(
        [extended[0:row_count], extended[1 : row_count + 1], extended[2 : row_count + 2]], axis=1
    )
    row_pick = (
        (lat_offsets + 1)[:, :, None] == jnp.arange(3, dtype=jnp.int32)[None, None, :]
    ).astype(jnp.float32)
    target = jnp.arange(col_count, dtype=jnp.int32)[None, None, :] + HW + lon_offsets[:, :, None]
    col_pick = (
        target[:, :, :, None] == jnp.arange(span, dtype=jnp.int32)[None, None, None, :]
    ).astype(jnp.float32)
    weights = jnp.einsum(
        "ikb,ikr,ikjq->bijrq", psi, row_pick, col_pick, precision=lax.Precision.HIGHEST
    )
    weights = weights.reshape(B, row_count, col_count, 3 * span)
    mix = jnp.einsum(
        "bijp,ipc->bijc", weights, stacked.astype(jnp.float32), precision=lax.Precision.HIGHEST
    )
    mix = mix.astype(jnp.bfloat16)
    inner = state.astype(jnp.float32).reshape(-1, width)
    for basis in range(B):
        inner = inner + jnp.dot(
            mix[basis].reshape(-1, width), w_disco[basis], preferred_element_type=jnp.float32
        )
    mean = jnp.mean(inner, axis=1, keepdims=True)
    centred = inner - mean
    variance = jnp.mean(centred * centred, axis=1, keepdims=True)
    normed = (centred * lax.rsqrt(variance + 1e-05) * norm_gain).astype(jnp.bfloat16)
    hidden = jax.nn.gelu(
        jnp.dot(normed, w_up, preferred_element_type=jnp.float32) + bias_up
    ).astype(jnp.bfloat16)
    result = inner + jnp.dot(hidden, w_down, preferred_element_type=jnp.float32)
    return result.astype(jnp.bfloat16).reshape(row_count, col_count, width)


def window_shards(
    analysis, noise, w_in, lat_offsets, lon_offsets, psi, w_disco, norm_gain, w_up, bias_up, w_down
):
    row_count, col_count, quarter = analysis.shape
    width = w_in.shape[1]
    start = lax.axis_index("member") * quarter
    own_rows = lax.dynamic_slice_in_dim(w_in, start, quarter, 0)
    partial_base = jnp.dot(
        analysis.reshape(-1, quarter), own_rows, preferred_element_type=jnp.float32
    )
    base = lax.psum(partial_base.astype(jnp.bfloat16), "member").astype(jnp.float32)
    state = (base + noise[0].reshape(-1, width).astype(jnp.float32)).astype(jnp.bfloat16)
    state = state.reshape(row_count, col_count, width)
    for step in range(PASSES):
        state = window_pass(
            state, lat_offsets, lon_offsets, psi, w_disco, norm_gain, w_up, bias_up, w_down
        )
    return state[None]


def border_kernel(border_ref):
    border_ref[...] = jnp.zeros_like(border_ref)


def weights_kernel(
    lat_ref, lon_ref, psi_ref, w_in_ref, w_disco_ref, w_up_ref, w_down_ref, gain_ref, bias_ref,
    weights_ref, spread_ref, disco_out, up_out, down_out, gain_out, bias_out, in_ref, sems,
):
    pairs = (
        (w_in_ref, in_ref), (w_disco_ref, disco_out), (w_up_ref, up_out),
        (w_down_ref, down_out), (gain_ref, gain_out), (bias_ref, bias_out),
    )
    copies = [
        pltpu.make_async_copy(source, target, sems.at[i]) for i, (source, target) in enumerate(pairs)
    ]
    for copy in copies:
        copy.start()
    f32 = jnp.float32
    rows = lat_ref.shape[1]
    band = lax.axis_index("lat")
    row = lax.broadcasted_iota(jnp.int32, (K, rows), 1)
    up, along = lat_ref[...], lon_ref[...]
    crossing = ((band == 0) & (row == 0) & (up < 0)) | (
        (band == lax.axis_size("lat") - 1) & (row == rows - 1) & (up > 0)
    )
    place = jnp.where(crossing, 1, up + 1) * 16 + ((along + jnp.where(crossing, 8, 0)) & 15)
    spot = lax.broadcasted_iota(jnp.int32, (48, rows), 0)
    sums = [jnp.zeros((48, rows), f32) for _ in range(B)]
    for k in range(K):
        hit = spot == place[k : k + 1]
        for b in range(B):
            sums[b] = sums[b] + jnp.where(hit, psi_ref[k, b : b + 1, :], 0.0)
    lines = [
        jnp.transpose(jnp.pad(part, ((0, 80), (0, 128 - rows))))[:rows] for part in sums
    ]
    col = lax.broadcasted_iota(jnp.int32, (16, 128), 0)
    straight = lax.broadcasted_iota(jnp.int32, (16, 128), 1) % 16 >= col
    for i in range(rows):
        shift = (i + 1) % GROUP * 16
        for b in range(B):
            line = jnp.broadcast_to(lines[b][i : i + 1], (16, 128))
            turned = jnp.where(
                straight,
                pltpu.roll(line, shift, 1, stride=1, stride_axis=0),
                pltpu.roll(line, (shift + 112) % 128, 1, stride=1, stride_axis=0),
            )
            weights_ref[pl.ds((i * B + b) * 16, 16), :] = turned.astype(jnp.bfloat16)
    member = lax.axis_index("member")
    quarter = w_in_ref.shape[0] // 4
    copies[0].wait()
    even = member - member % 2
    groups = (
        member, member ^ 1, member ^ 2, member ^ 3, even, even ^ 1, even ^ 3, even ^ 2
    )
    for place, group in enumerate(groups):
        spread_ref[pl.ds(place * quarter, quarter), :] = in_ref[
            pl.ds(pl.multiple_of(group * quarter, quarter), quarter), :
        ]
    for copy in copies[1:]:
        copy.wait()


def start_kernel(
    chip_ref, x_ref, sent_ref, got_ref, noise_ref, from_y_ref, spread_ref, weights_ref, border_ref,
    state_ref, first_ref, second_ref,
):
    f32, bf16 = jnp.float32, jnp.bfloat16
    rows, cols, width = noise_ref.shape
    wide = lambda block: block.astype(f32).reshape(rows * cols, block.shape[2])
    sent, got = wide(sent_ref[...]), wide(got_ref[...])
    even_core = lax.axis_index("member") % 2 == 0
    along_y, diagonal = jnp.where(even_core, sent, got), jnp.where(even_core, got, sent)

    def base_of(parts, first):
        analysis = jnp.concatenate(parts, axis=1).astype(bf16)
        base = jnp.dot(
            analysis, spread_ref[pl.ds(first, analysis.shape[1]), :], preferred_element_type=f32
        )
        return base.reshape(rows, cols, width)

    own = base_of([wide(chip_ref[pl.ds(0, rows)]), wide(x_ref[pl.ds(0, rows)])], 0)
    other = base_of([along_y, diagonal], width)
    state = jnp.concatenate(
        [own + noise_ref[...].astype(f32), other + from_y_ref[...].astype(f32)], axis=1
    )
    state = state.astype(bf16).reshape(rows * 16, width)
    state_ref[pl.ds(0, 32), :] = border_ref[...]
    state_ref[pl.ds(32, rows * 16), :] = state
    state_ref[pl.ds(32 + rows * 16, 32), :] = border_ref[...]
    even = lax.axis_index("lat") % 2 == 0
    for ref, last in ((first_ref, even), (second_ref, jnp.logical_not(even))):
        line = pl.multiple_of(jnp.where(last, (rows - 1) * B * 16, 0), 16)
        cell = pl.multiple_of(jnp.where(last, rows * 16, 32), 16)
        ref[pl.ds(0, 32), :] = state_ref[pl.ds(cell, 32), pl.ds(0, 128)]
        ref[pl.ds(32, 32), :] = state_ref[pl.ds(cell, 32), pl.ds(128, 128)]
        ref[pl.ds(64, B * 16), :] = weights_ref[pl.ds(line, B * 16), :]


def mixed(weights, state, count, width):
    mix = jnp.dot(weights, state, preferred_element_type=jnp.float32)
    return mix.reshape(count, B, 16, width)


def cell_block(before, mix, w_disco_ref, gain_ref, w_up_ref, bias_ref, w_down_ref):
    f32, bf16 = jnp.float32, jnp.bfloat16
    width = before.shape[1]
    inner = before + jnp.dot(
        mix, w_disco_ref[...].reshape(B * width, width), preferred_element_type=f32
    )
    mean = jnp.mean(inner, axis=1, keepdims=True)
    variance = jnp.mean(inner * inner, axis=1, keepdims=True) - mean * mean
    scale = lax.rsqrt(jnp.maximum(variance, 0.0) + 1e-05)
    normed = ((inner - mean) * scale * gain_ref[...]).astype(bf16)
    hidden = jax.nn.gelu(
        jnp.dot(normed, w_up_ref[...], preferred_element_type=f32) + bias_ref[...]
    ).astype(bf16)
    return inner + jnp.dot(hidden, w_down_ref[...], preferred_element_type=f32)


def mixed_rows(low, high, rows, weights_ref, state_ref):
    first = low - low % GROUP
    reach = min(GROUP + 2, rows + 4 - first) * 16
    return mixed(
        weights_ref[pl.ds((low - 1) * B * 16, (high - low) * B * 16), pl.ds(0, reach)],
        state_ref[pl.ds(first * 16, reach), :],
        high - low,
        state_ref.shape[1],
    )


def inner_kernel(
    state_ref, weights_ref, w_disco_ref, gain_ref, w_up_ref, bias_ref, w_down_ref,
    near_ref, out_ref, next_ref, mix_ref, own_mix_ref,
):
    f32, bf16 = jnp.float32, jnp.bfloat16
    width = state_ref.shape[1]
    rows, cols = out_ref.shape[0] + 4, out_ref.shape[1]
    block = functools.partial(
        cell_block, w_disco_ref=w_disco_ref, gain_ref=gain_ref, w_up_ref=w_up_ref,
        bias_ref=bias_ref, w_down_ref=w_down_ref,
    )
    for first in range(0, rows, GROUP):
        low, high = max(first, 2), min(first + GROUP, rows)
        mix = mixed_rows(low, high, rows, weights_ref, state_ref)
        for i in range(low, high):
            for b in range(B):
                mix_ref[pl.ds((i - 2) * 16, 16), pl.ds(b * width, width)] = mix[i - low, b].astype(bf16)
    after = block(
        state_ref[pl.ds(48, (rows - 2) * 16), :].astype(f32), mix_ref[...]
    ).astype(bf16)
    border = jnp.zeros((48, width), bf16)
    next_ref[pl.ds(0, 48), :] = border
    next_ref[pl.ds(48, (rows - 2) * 16), :] = after
    next_ref[pl.ds(16 + rows * 16, 48), :] = border
    near_ref[pl.ds(0, 32), :] = after[:32]
    near_ref[pl.ds(32, 32), :] = after[(rows - 4) * 16 :]
    for first in range(0, rows - 1, GROUP):
        low, high = max(first, 3), min(first + GROUP, rows - 1)
        mix = mixed_rows(low, high, rows, weights_ref, next_ref)
        for i in range(low, high):
            for b in range(B):
                own_mix_ref[pl.ds((i - 3) * cols, cols), pl.ds(b * width, width)] = mix[i - low, b, :cols]
    own = next_ref[pl.ds(64, (rows - 4) * 16), :].astype(f32).reshape(rows - 4, 16, width)[:, :cols]
    result = block(own.reshape((rows - 4) * cols, width), own_mix_ref[...].astype(bf16))
    out_ref[...] = result.reshape(rows - 4, cols, width).astype(bf16)


def edge_kernel(
    state_ref, near_ref, inner_ref, first_ref, second_ref, weights_ref,
    w_disco_ref, gain_ref, w_up_ref, bias_ref, w_down_ref, out_ref, next_ref, halo_ref, last_ref, sems,
):
    f32, bf16 = jnp.float32, jnp.bfloat16
    rows, cols, width = out_ref.shape
    block = functools.partial(
        cell_block, w_disco_ref=w_disco_ref, gain_ref=gain_ref, w_up_ref=w_up_ref,
        bias_ref=bias_ref, w_down_ref=w_down_ref,
    )
    inner_copy = pltpu.make_async_copy(inner_ref, out_ref.at[pl.ds(2, rows - 4)], sems.at[0])
    inner_copy.start()
    line = B * 16
    even = lax.axis_index("lat") % 2 == 0
    halo_ref[jnp.where(even, 1, 0)] = first_ref[...]
    halo_ref[jnp.where(even, 0, 1)] = second_ref[...]

    def received(side):
        return jnp.concatenate([halo_ref[side, :32, :], halo_ref[side, 32:64, :]], axis=1)

    def one_row(mix):
        return jnp.concatenate([mix[b] for b in range(B)], axis=1)

    top_state = jnp.concatenate([received(0), state_ref[pl.ds(32, 32), :]], axis=0)
    top_mix = mixed(
        jnp.concatenate([halo_ref[0, 64:, :], weights_ref[pl.ds(0, line), :]], axis=0)[:, :64],
        top_state, 2, width,
    )
    bottom_state = jnp.concatenate(
        [state_ref[pl.ds(rows * 16, 32), :], received(1)], axis=0
    )
    bottom_mix = mixed(
        jnp.concatenate(
            [weights_ref[pl.ds((rows - 1) * line, line), :], halo_ref[1, 64:, :]], axis=0
        )[:, :64],
        bottom_state, 2, width,
    )
    edge_mix = jnp.concatenate(
        [one_row(mix[i]) for mix in (top_mix, bottom_mix) for i in range(2)], axis=0
    ).astype(bf16)
    edge_state = jnp.concatenate([top_state[16:48], bottom_state[16:48]], axis=0)
    edge = block(edge_state.astype(f32), edge_mix).astype(bf16)
    next_ref[...] = jnp.zeros_like(next_ref)
    next_ref[pl.ds(16, 32), :] = edge[:32]
    next_ref[pl.ds(48, 32), :] = near_ref[pl.ds(0, 32), :]
    next_ref[pl.ds((rows - 1) * 16, 32), :] = near_ref[pl.ds(32, 32), :]
    next_ref[pl.ds((rows + 1) * 16, 32), :] = edge[32:]
    mixes, own = [], []
    for low, high in ((1, 3), (rows - 1, rows), (rows, rows + 1)):
        mix = mixed_rows(low, high, rows, weights_ref, next_ref)
        for i in range(low, high):
            mixes.append(one_row(mix[i - low, :, :cols]))
            own.append(next_ref[pl.ds((i + 1) * 16, 16), :].astype(f32)[:cols])
    result = block(jnp.concatenate(own, axis=0), jnp.concatenate(mixes, axis=0).astype(bf16))
    last_ref[...] = result.reshape(4, cols, width).astype(bf16)
    top_copy = pltpu.make_async_copy(
        last_ref.at[pl.ds(0, 2)], out_ref.at[pl.ds(0, 2)], sems.at[1]
    )
    bottom_copy = pltpu.make_async_copy(
        last_ref.at[pl.ds(2, 2)], out_ref.at[pl.ds(rows - 2, 2)], sems.at[2]
    )
    top_copy.start()
    bottom_copy.start()
    inner_copy.wait()
    top_copy.wait()
    bottom_copy.wait()


def circle_shards(
    analysis, noise, w_in, lat_offsets, lon_offsets, psi, w_disco, norm_gain, w_up, bias_up, w_down
):
    f32, bf16 = jnp.float32, jnp.bfloat16
    rows, cols, quarter = analysis.shape
    width = w_in.shape[1]
    noise = noise[0]
    bands = lax.axis_size("lat")
    members = lax.axis_size("member")
    line = B * 16
    vmem = pl.BlockSpec(memory_space=pltpu.VMEM)
    hbm = pl.BlockSpec(memory_space=pltpu.HBM)
    params = pltpu.CompilerParams(vmem_limit_bytes=12 * 1024 * 1024)

    def shape(*dims, dtype=bf16):
        return jax.ShapeDtypeStruct(dims, dtype)

    def swapped(block, partner):
        pairs = [(i, partner(i)) for i in range(2 * members)]
        return lax.ppermute(block, ("member", "lon"), pairs)

    from_y = swapped(noise, lambda i: i ^ 1)
    from_core = swapped(analysis, lambda i: i ^ 2)
    border = pl.pallas_call(
        border_kernel,
        out_shape=shape(32, width),
        out_specs=vmem,
        cost_estimate=pl.CostEstimate(flops=1_000_000_000, bytes_accessed=16_384, transcendentals=0),
        compiler_params=params,
    )()
    analysis, border = lax.optimization_barrier((analysis, border))
    chip = jnp.pad(jnp.concatenate([analysis, from_core], axis=2), ((0, 1), (0, 0), (0, 0)))
    across = swapped(chip, lambda i: i ^ 5 if i & 2 else i ^ 1)
    from_x = swapped(chip, lambda i: i ^ 4)
    weights, spread, *dense = pl.pallas_call(
        weights_kernel,
        out_shape=(
            shape(rows * line, 128), shape(8 * quarter, width), shape(*w_disco.shape),
            shape(*w_up.shape), shape(*w_down.shape), shape(1, width, dtype=f32),
            shape(1, w_up.shape[1], dtype=f32),
        ),
        in_specs=[vmem] * 3 + [hbm] * 6,
        out_specs=(vmem,) * 7,
        scratch_shapes=[pltpu.VMEM(w_in.shape, bf16), pltpu.SemaphoreType.DMA((6,))],
        cost_estimate=pl.CostEstimate(flops=4_000, bytes_accessed=3_000, transcendentals=0),
        compiler_params=params,
    )(
        lat_offsets.T,
        lon_offsets.T,
        jnp.transpose(psi, (1, 2, 0)),
        *(
            pltpu.with_memory_space_constraint(w, pltpu.HBM)
            for w in (
                w_in, w_disco, w_up, w_down, norm_gain.reshape(1, -1), bias_up.reshape(1, -1)
            )
        ),
    )
    w_disco, w_up, w_down, norm_gain, bias_up = dense
    dense = (w_disco, norm_gain, w_up, bias_up, w_down)

    across, from_y, weights = lax.optimization_barrier((across, from_y, weights))
    across = across[:rows]
    got = swapped(across, lambda i: i ^ 2)
    state, first, second = pl.pallas_call(
        start_kernel,
        out_shape=(shape((rows + 4) * 16, width), shape(64 + line, 128), shape(64 + line, 128)),
        in_specs=[vmem] * 9,
        out_specs=(vmem,) * 3,
        cost_estimate=pl.CostEstimate(flops=200_000_000, bytes_accessed=1_000_000, transcendentals=0),
        compiler_params=params,
    )(chip, from_x, across, got, noise, from_y, spread, weights, border)
    def paired(edge, start):
        pairs = []
        for i in range(members):
            for j in range(bands):
                k = j + 1 if (j - start) % 2 == 0 else j - 1
                there = (i, k) if min(j, k) >= start and k < bands else (i ^ 1, j)
                pairs.append((i * bands + j, there[0] * bands + there[1]))
        return lax.ppermute(edge, ("member", "lat"), pairs)

    first, second = paired(first, 0), paired(second, 1)
    near, inner = pl.pallas_call(
        inner_kernel,
        out_shape=(shape(64, width), shape(rows - 4, cols, width)),
        in_specs=[vmem] * 7,
        out_specs=(vmem, vmem),
        scratch_shapes=[
            pltpu.VMEM(((rows + 4) * 16, width), bf16),
            pltpu.VMEM(((rows - 2) * 16, B * width), bf16),
            pltpu.VMEM(((rows - 4) * cols, B * width), f32),
        ],
        cost_estimate=pl.CostEstimate(
            flops=800_000_000, bytes_accessed=2_000_000, transcendentals=400_000
        ),
        compiler_params=params,
    )(state, weights, *dense)
    result = pl.pallas_call(
        edge_kernel,
        out_shape=shape(rows, cols, width),
        in_specs=[vmem] * 11,
        out_specs=pl.BlockSpec(memory_space=pl.ANY),
        scratch_shapes=[
            pltpu.VMEM(((rows + 4) * 16, width), bf16),
            pltpu.VMEM((2, 64 + line, 128), bf16),
            pltpu.VMEM((4, cols, width), bf16),
            pltpu.SemaphoreType.DMA((3,)),
        ],
        cost_estimate=pl.CostEstimate(
            flops=100_000_000, bytes_accessed=2_000_000, transcendentals=50_000
        ),
        compiler_params=params,
    )(state, near, inner, first, second, weights, *dense)
    return result[None]


def solution(mesh):
    circle = mesh.shape["lon"] == 2 and mesh.shape["member"] == 4
    return jax.shard_map(
        circle_shards if circle else window_shards,
        mesh=mesh,
        in_specs=(
            P("lat", "lon", "member"),
            P("member", "lat", "lon", None),
            P(),
            P("lat", None),
            P("lat", None),
            P("lat", None, None),
            P(),
            P(),
            P(),
            P(),
            P(),
        ),
        out_specs=P("member", "lat", "lon", None),
        check_vma=False,
    )
```

```python
import functools

import jax
import jax.numpy as jnp
from jax import lax
from jax.experimental import pallas as pl
from jax.experimental.pallas import tpu as pltpu
from jax.sharding import PartitionSpec as P

B = 3
HW = 8
PASSES = 2
K = 9
GROUP = 6


def ring_padded(cells, sides, width, closed):
    for axis, dim in sides:
        count = lax.axis_size(axis)
        ends = count if closed else count - 1
        head = lax.slice_in_dim(cells, 0, width, axis=dim)
        tail = lax.slice_in_dim(cells, cells.shape[dim] - width, cells.shape[dim], axis=dim)
        cells = jnp.concatenate(
            [
                lax.ppermute(tail, axis, [(i, (i + 1) % count) for i in range(ends)]),
                cells,
                lax.ppermute(head, axis, [((i + 1) % count, i) for i in range(ends)]),
            ],
            axis=dim,
        )
    return cells


def extend(state):
    count = lax.axis_size("lon")
    rows = ring_padded(state, (("lat", 0),), 1, False)
    edges = jnp.stack([state[0], state[-1]])
    flipped = lax.ppermute(edges, "lon", [(i, (i + count // 2) % count) for i in range(count)])
    band = lax.axis_index("lat")
    last_band = lax.axis_size("lat") - 1
    top = jnp.where(band == 0, flipped[0], rows[0])
    bottom = jnp.where(band == last_band, flipped[1], rows[-1])
    rows = jnp.concatenate([top[None], rows[1:-1], bottom[None]], axis=0)
    return ring_padded(rows, (("lon", 1),), HW, True)


def window_pass(state, lat_offsets, lon_offsets, psi, w_disco, norm_gain, w_up, bias_up, w_down):
    row_count, col_count, width = state.shape
    extended = extend(state)
    span = col_count + 2 * HW
    stacked = jnp.concatenate(
        [extended[0:row_count], extended[1 : row_count + 1], extended[2 : row_count + 2]], axis=1
    )
    row_pick = (
        (lat_offsets + 1)[:, :, None] == jnp.arange(3, dtype=jnp.int32)[None, None, :]
    ).astype(jnp.float32)
    target = jnp.arange(col_count, dtype=jnp.int32)[None, None, :] + HW + lon_offsets[:, :, None]
    col_pick = (
        target[:, :, :, None] == jnp.arange(span, dtype=jnp.int32)[None, None, None, :]
    ).astype(jnp.float32)
    weights = jnp.einsum(
        "ikb,ikr,ikjq->bijrq", psi, row_pick, col_pick, precision=lax.Precision.HIGHEST
    )
    weights = weights.reshape(B, row_count, col_count, 3 * span)
    mix = jnp.einsum(
        "bijp,ipc->bijc", weights, stacked.astype(jnp.float32), precision=lax.Precision.HIGHEST
    )
    mix = mix.astype(jnp.bfloat16)
    inner = state.astype(jnp.float32).reshape(-1, width)
    for basis in range(B):
        inner = inner + jnp.dot(
            mix[basis].reshape(-1, width), w_disco[basis], preferred_element_type=jnp.float32
        )
    mean = jnp.mean(inner, axis=1, keepdims=True)
    centred = inner - mean
    variance = jnp.mean(centred * centred, axis=1, keepdims=True)
    normed = (centred * lax.rsqrt(variance + 1e-05) * norm_gain).astype(jnp.bfloat16)
    hidden = jax.nn.gelu(
        jnp.dot(normed, w_up, preferred_element_type=jnp.float32) + bias_up
    ).astype(jnp.bfloat16)
    result = inner + jnp.dot(hidden, w_down, preferred_element_type=jnp.float32)
    return result.astype(jnp.bfloat16).reshape(row_count, col_count, width)


def window_shards(
    analysis, noise, w_in, lat_offsets, lon_offsets, psi, w_disco, norm_gain, w_up, bias_up, w_down
):
    row_count, col_count, quarter = analysis.shape
    width = w_in.shape[1]
    start = lax.axis_index("member") * quarter
    own_rows = lax.dynamic_slice_in_dim(w_in, start, quarter, 0)
    partial_base = jnp.dot(
        analysis.reshape(-1, quarter), own_rows, preferred_element_type=jnp.float32
    )
    base = lax.psum(partial_base.astype(jnp.bfloat16), "member").astype(jnp.float32)
    state = (base + noise[0].reshape(-1, width).astype(jnp.float32)).astype(jnp.bfloat16)
    state = state.reshape(row_count, col_count, width)
    for step in range(PASSES):
        state = window_pass(
            state, lat_offsets, lon_offsets, psi, w_disco, norm_gain, w_up, bias_up, w_down
        )
    return state[None]


def border_kernel(border_ref):
    border_ref[...] = jnp.zeros_like(border_ref)


def weights_kernel(
    lat_ref, lon_ref, psi_ref, w_in_ref, w_disco_ref, w_up_ref, w_down_ref, gain_ref, bias_ref,
    weights_ref, spread_ref, disco_out, up_out, down_out, gain_out, bias_out, in_ref, sems,
):
    pairs = (
        (w_in_ref, in_ref), (w_disco_ref, disco_out), (w_up_ref, up_out),
        (w_down_ref, down_out), (gain_ref, gain_out), (bias_ref, bias_out),
    )
    copies = [
        pltpu.make_async_copy(source, target, sems.at[i]) for i, (source, target) in enumerate(pairs)
    ]
    for copy in copies:
        copy.start()
    f32 = jnp.float32
    rows = lat_ref.shape[1]
    band = lax.axis_index("lat")
    row = lax.broadcasted_iota(jnp.int32, (K, rows), 1)
    up, along = lat_ref[...], lon_ref[...]
    crossing = ((band == 0) & (row == 0) & (up < 0)) | (
        (band == lax.axis_size("lat") - 1) & (row == rows - 1) & (up > 0)
    )
    place = jnp.where(crossing, 1, up + 1) * 16 + ((along + jnp.where(crossing, 8, 0)) & 15)
    spot = lax.broadcasted_iota(jnp.int32, (48, rows), 0)
    sums = [jnp.zeros((48, rows), f32) for _ in range(B)]
    for k in range(K):
        hit = spot == place[k : k + 1]
        for b in range(B):
            sums[b] = sums[b] + jnp.where(hit, psi_ref[k, b : b + 1, :], 0.0)
    lines = [
        jnp.transpose(jnp.pad(part, ((0, 80), (0, 128 - rows))))[:rows] for part in sums
    ]
    col = lax.broadcasted_iota(jnp.int32, (16, 128), 0)
    straight = lax.broadcasted_iota(jnp.int32, (16, 128), 1) % 16 >= col
    for i in range(rows):
        shift = (i + 1) % GROUP * 16
        for b in range(B):
            line = jnp.broadcast_to(lines[b][i : i + 1], (16, 128))
            turned = jnp.where(
                straight,
                pltpu.roll(line, shift, 1, stride=1, stride_axis=0),
                pltpu.roll(line, (shift + 112) % 128, 1, stride=1, stride_axis=0),
            )
            weights_ref[pl.ds((i * B + b) * 16, 16), :] = turned.astype(jnp.bfloat16)
    member = lax.axis_index("member")
    quarter = w_in_ref.shape[0] // 4
    copies[0].wait()
    even = member - member % 2
    groups = (
        member, member ^ 1, member ^ 2, member ^ 3, even, even ^ 1, even ^ 3, even ^ 2
    )
    for place, group in enumerate(groups):
        spread_ref[pl.ds(place * quarter, quarter), :] = in_ref[
            pl.ds(pl.multiple_of(group * quarter, quarter), quarter), :
        ]
    for copy in copies[1:]:
        copy.wait()


def start_kernel(
    chip_ref, x_ref, sent_ref, got_ref, noise_ref, from_y_ref, spread_ref, weights_ref, border_ref,
    state_ref, first_ref, second_ref,
):
    f32, bf16 = jnp.float32, jnp.bfloat16
    rows, cols, width = noise_ref.shape
    wide = lambda block: block.astype(f32).reshape(rows * cols, block.shape[2])
    sent, got = wide(sent_ref[...]), wide(got_ref[...])
    even_core = lax.axis_index("member") % 2 == 0
    along_y, diagonal = jnp.where(even_core, sent, got), jnp.where(even_core, got, sent)

    def base_of(parts, first):
        analysis = jnp.concatenate(parts, axis=1).astype(bf16)
        base = jnp.dot(
            analysis, spread_ref[pl.ds(first, analysis.shape[1]), :], preferred_element_type=f32
        )
        return base.reshape(rows, cols, width)

    own = base_of([wide(chip_ref[pl.ds(0, rows)]), wide(x_ref[pl.ds(0, rows)])], 0)
    other = base_of([along_y, diagonal], width)
    state = jnp.concatenate(
        [own + noise_ref[...].astype(f32), other + from_y_ref[...].astype(f32)], axis=1
    )
    state = state.astype(bf16).reshape(rows * 16, width)
    state_ref[pl.ds(0, 32), :] = border_ref[...]
    state_ref[pl.ds(32, rows * 16), :] = state
    state_ref[pl.ds(32 + rows * 16, 32), :] = border_ref[...]
    even = lax.axis_index("lat") % 2 == 0
    for ref, last in ((first_ref, even), (second_ref, jnp.logical_not(even))):
        line = pl.multiple_of(jnp.where(last, (rows - 1) * B * 16, 0), 16)
        cell = pl.multiple_of(jnp.where(last, rows * 16, 32), 16)
        ref[pl.ds(0, 32), :] = state_ref[pl.ds(cell, 32), pl.ds(0, 128)]
        ref[pl.ds(32, 32), :] = state_ref[pl.ds(cell, 32), pl.ds(128, 128)]
        ref[pl.ds(64, B * 16), :] = weights_ref[pl.ds(line, B * 16), :]


def mixed(weights, state, count, width):
    mix = jnp.dot(weights, state, preferred_element_type=jnp.float32)
    return mix.reshape(count, B, 16, width)


def product(left, right_ref, pieces):
    wide = right_ref.shape[1] // pieces
    return jnp.concatenate(
        [
            jnp.dot(left, right_ref[:, pl.ds(i * wide, wide)], preferred_element_type=jnp.float32)
            for i in range(pieces)
        ],
        axis=1,
    )


def cell_block(before, mix, w_disco_ref, gain_ref, w_up_ref, bias_ref, w_down_ref, pieces=1):
    bf16 = jnp.bfloat16
    inner = before + product(mix, w_disco_ref, pieces)
    mean = jnp.mean(inner, axis=1, keepdims=True)
    variance = jnp.mean(inner * inner, axis=1, keepdims=True) - mean * mean
    scale = lax.rsqrt(jnp.maximum(variance, 0.0) + 1e-05)
    normed = ((inner - mean) * scale * gain_ref[...]).astype(bf16)
    hidden = jax.nn.gelu(product(normed, w_up_ref, pieces) + bias_ref[...]).astype(bf16)
    return inner + product(hidden, w_down_ref, pieces)


def mixed_rows(low, high, rows, weights_ref, state_ref):
    first = low - low % GROUP
    reach = min(GROUP + 2, rows + 4 - first) * 16
    return mixed(
        weights_ref[pl.ds((low - 1) * B * 16, (high - low) * B * 16), pl.ds(0, reach)],
        state_ref[pl.ds(first * 16, reach), :],
        high - low,
        state_ref.shape[1],
    )


def inner_kernel(
    state_ref, weights_ref, w_disco_ref, gain_ref, w_up_ref, bias_ref, w_down_ref,
    near_ref, out_ref, next_ref, mix_ref, own_mix_ref,
):
    f32, bf16 = jnp.float32, jnp.bfloat16
    width = state_ref.shape[1]
    rows, cols = out_ref.shape[0] + 4, out_ref.shape[1]
    block = functools.partial(
        cell_block, w_disco_ref=w_disco_ref, gain_ref=gain_ref, w_up_ref=w_up_ref,
        bias_ref=bias_ref, w_down_ref=w_down_ref,
    )
    for first in range(0, rows, GROUP):
        low, high = max(first, 2), min(first + GROUP, rows)
        mix = mixed_rows(low, high, rows, weights_ref, state_ref)
        for i in range(low, high):
            for b in range(B):
                mix_ref[pl.ds((i - 2) * 16, 16), pl.ds(b * width, width)] = mix[i - low, b].astype(bf16)
    after = block(
        state_ref[pl.ds(48, (rows - 2) * 16), :].astype(f32), mix_ref[...]
    ).astype(bf16)
    border = jnp.zeros((48, width), bf16)
    next_ref[pl.ds(0, 48), :] = border
    next_ref[pl.ds(48, (rows - 2) * 16), :] = after
    next_ref[pl.ds(16 + rows * 16, 48), :] = border
    near_ref[pl.ds(0, 32), :] = after[:32]
    near_ref[pl.ds(32, 32), :] = after[(rows - 4) * 16 :]
    for first in range(0, rows - 1, GROUP):
        low, high = max(first, 3), min(first + GROUP, rows - 1)
        mix = mixed_rows(low, high, rows, weights_ref, next_ref)
        for i in range(low, high):
            for b in range(B):
                own_mix_ref[pl.ds((i - 3) * cols, cols), pl.ds(b * width, width)] = mix[i - low, b, :cols]
    own = next_ref[pl.ds(64, (rows - 4) * 16), :].astype(f32).reshape(rows - 4, 16, width)[:, :cols]
    result = block(own.reshape((rows - 4) * cols, width), own_mix_ref[...].astype(bf16))
    out_ref[...] = result.reshape(rows - 4, cols, width).astype(bf16)


def edge_kernel(
    state_ref, near_ref, inner_ref, first_ref, second_ref, weights_ref,
    w_disco_ref, gain_ref, w_up_ref, bias_ref, w_down_ref, out_ref, next_ref, halo_ref, last_ref, sems,
):
    f32, bf16 = jnp.float32, jnp.bfloat16
    rows, cols, width = out_ref.shape
    block = functools.partial(
        cell_block, w_disco_ref=w_disco_ref, gain_ref=gain_ref, w_up_ref=w_up_ref,
        bias_ref=bias_ref, w_down_ref=w_down_ref, pieces=2,
    )
    inner_copy = pltpu.make_async_copy(inner_ref, out_ref.at[pl.ds(2, rows - 4)], sems.at[0])
    inner_copy.start()
    line = B * 16
    even = lax.axis_index("lat") % 2 == 0
    halo_ref[jnp.where(even, 1, 0)] = first_ref[...]
    halo_ref[jnp.where(even, 0, 1)] = second_ref[...]

    def received(side):
        return jnp.concatenate([halo_ref[side, :32, :], halo_ref[side, 32:64, :]], axis=1)

    def one_row(mix):
        return jnp.concatenate([mix[b] for b in range(B)], axis=1)

    top_state = jnp.concatenate([received(0), state_ref[pl.ds(32, 32), :]], axis=0)
    top_mix = mixed(
        jnp.concatenate([halo_ref[0, 64:, :], weights_ref[pl.ds(0, line), :]], axis=0)[:, :64],
        top_state, 2, width,
    )
    bottom_state = jnp.concatenate(
        [state_ref[pl.ds(rows * 16, 32), :], received(1)], axis=0
    )
    bottom_mix = mixed(
        jnp.concatenate(
            [weights_ref[pl.ds((rows - 1) * line, line), :], halo_ref[1, 64:, :]], axis=0
        )[:, :64],
        bottom_state, 2, width,
    )
    edge_mix = jnp.concatenate(
        [one_row(mix[i]) for mix in (top_mix, bottom_mix) for i in range(2)], axis=0
    ).astype(bf16)
    edge_state = jnp.concatenate([top_state[16:48], bottom_state[16:48]], axis=0)
    edge = block(edge_state.astype(f32), edge_mix).astype(bf16)
    next_ref[...] = jnp.zeros_like(next_ref)
    next_ref[pl.ds(16, 32), :] = edge[:32]
    next_ref[pl.ds(48, 32), :] = near_ref[pl.ds(0, 32), :]
    next_ref[pl.ds((rows - 1) * 16, 32), :] = near_ref[pl.ds(32, 32), :]
    next_ref[pl.ds((rows + 1) * 16, 32), :] = edge[32:]
    mixes, own = [], []
    for low, high in ((1, 3), (rows - 1, rows), (rows, rows + 1)):
        mix = mixed_rows(low, high, rows, weights_ref, next_ref)
        for i in range(low, high):
            mixes.append(one_row(mix[i - low, :, :cols]))
            own.append(next_ref[pl.ds((i + 1) * 16, 16), :].astype(f32)[:cols])
    result = block(jnp.concatenate(own, axis=0), jnp.concatenate(mixes, axis=0).astype(bf16))
    last_ref[...] = result.reshape(4, cols, width).astype(bf16)
    top_copy = pltpu.make_async_copy(
        last_ref.at[pl.ds(0, 2)], out_ref.at[pl.ds(0, 2)], sems.at[1]
    )
    bottom_copy = pltpu.make_async_copy(
        last_ref.at[pl.ds(2, 2)], out_ref.at[pl.ds(rows - 2, 2)], sems.at[2]
    )
    top_copy.start()
    bottom_copy.start()
    inner_copy.wait()
    top_copy.wait()
    bottom_copy.wait()


def circle_shards(
    analysis, noise, w_in, lat_offsets, lon_offsets, psi, w_disco, norm_gain, w_up, bias_up, w_down
):
    f32, bf16 = jnp.float32, jnp.bfloat16
    rows, cols, quarter = analysis.shape
    width = w_in.shape[1]
    noise = noise[0]
    w_disco = w_disco.reshape(B * width, width)
    bands = lax.axis_size("lat")
    members = lax.axis_size("member")
    line = B * 16
    vmem = pl.BlockSpec(memory_space=pltpu.VMEM)
    hbm = pl.BlockSpec(memory_space=pltpu.HBM)
    params = pltpu.CompilerParams(vmem_limit_bytes=12 * 1024 * 1024)

    def shape(*dims, dtype=bf16):
        return jax.ShapeDtypeStruct(dims, dtype)

    def swapped(block, partner):
        pairs = [(i, partner(i)) for i in range(2 * members)]
        return lax.ppermute(block, ("member", "lon"), pairs)

    from_y = swapped(noise, lambda i: i ^ 1)
    from_core = swapped(analysis, lambda i: i ^ 2)
    border = pl.pallas_call(
        border_kernel,
        out_shape=shape(32, width),
        out_specs=vmem,
        cost_estimate=pl.CostEstimate(flops=1_000_000_000, bytes_accessed=16_384, transcendentals=0),
        compiler_params=params,
    )()
    analysis, border = lax.optimization_barrier((analysis, border))
    chip = jnp.pad(jnp.concatenate([analysis, from_core], axis=2), ((0, 1), (0, 0), (0, 0)))
    across = swapped(chip, lambda i: i ^ 5 if i & 2 else i ^ 1)
    from_x = swapped(chip, lambda i: i ^ 4)
    weights, spread, *dense = pl.pallas_call(
        weights_kernel,
        out_shape=(
            shape(rows * line, 128), shape(8 * quarter, width), shape(*w_disco.shape),
            shape(*w_up.shape), shape(*w_down.shape), shape(1, width, dtype=f32),
            shape(1, w_up.shape[1], dtype=f32),
        ),
        in_specs=[vmem] * 3 + [hbm] * 6,
        out_specs=(vmem,) * 7,
        scratch_shapes=[pltpu.VMEM(w_in.shape, bf16), pltpu.SemaphoreType.DMA((6,))],
        cost_estimate=pl.CostEstimate(flops=4_000, bytes_accessed=3_000, transcendentals=0),
        compiler_params=params,
    )(
        lat_offsets.T,
        lon_offsets.T,
        jnp.transpose(psi, (1, 2, 0)),
        *(
            pltpu.with_memory_space_constraint(w, pltpu.HBM)
            for w in (
                w_in, w_disco, w_up, w_down, norm_gain.reshape(1, -1), bias_up.reshape(1, -1)
            )
        ),
    )
    w_disco, w_up, w_down, norm_gain, bias_up = dense
    dense = (w_disco, norm_gain, w_up, bias_up, w_down)

    across, from_y, weights = lax.optimization_barrier((across, from_y, weights))
    across = across[:rows]
    got = swapped(across, lambda i: i ^ 2)
    state, first, second = pl.pallas_call(
        start_kernel,
        out_shape=(shape((rows + 4) * 16, width), shape(64 + line, 128), shape(64 + line, 128)),
        in_specs=[vmem] * 9,
        out_specs=(vmem,) * 3,
        cost_estimate=pl.CostEstimate(flops=200_000_000, bytes_accessed=1_000_000, transcendentals=0),
        compiler_params=params,
    )(chip, from_x, across, got, noise, from_y, spread, weights, border)
    def paired(edge, start):
        pairs = []
        for i in range(members):
            for j in range(bands):
                k = j + 1 if (j - start) % 2 == 0 else j - 1
                there = (i, k) if min(j, k) >= start and k < bands else (i ^ 1, j)
                pairs.append((i * bands + j, there[0] * bands + there[1]))
        return lax.ppermute(edge, ("member", "lat"), pairs)

    first, second = paired(first, 0), paired(second, 1)
    near, inner = pl.pallas_call(
        inner_kernel,
        out_shape=(shape(64, width), shape(rows - 4, cols, width)),
        in_specs=[vmem] * 7,
        out_specs=(vmem, vmem),
        scratch_shapes=[
            pltpu.VMEM(((rows + 4) * 16, width), bf16),
            pltpu.VMEM(((rows - 2) * 16, B * width), bf16),
            pltpu.VMEM(((rows - 4) * cols, B * width), f32),
        ],
        cost_estimate=pl.CostEstimate(
            flops=800_000_000, bytes_accessed=2_000_000, transcendentals=400_000
        ),
        compiler_params=params,
    )(state, weights, *dense)
    result = pl.pallas_call(
        edge_kernel,
        out_shape=shape(rows, cols, width),
        in_specs=[vmem] * 11,
        out_specs=pl.BlockSpec(memory_space=pl.ANY),
        scratch_shapes=[
            pltpu.VMEM(((rows + 4) * 16, width), bf16),
            pltpu.VMEM((2, 64 + line, 128), bf16),
            pltpu.VMEM((4, cols, width), bf16),
            pltpu.SemaphoreType.DMA((3,)),
        ],
        cost_estimate=pl.CostEstimate(
            flops=100_000_000, bytes_accessed=2_000_000, transcendentals=50_000
        ),
        compiler_params=params,
    )(state, near, inner, first, second, weights, *dense)
    return result[None]


def solution(mesh):
    circle = mesh.shape["lon"] == 2 and mesh.shape["member"] == 4
    return jax.shard_map(
        circle_shards if circle else window_shards,
        mesh=mesh,
        in_specs=(
            P("lat", "lon", "member"),
            P("member", "lat", "lon", None),
            P(),
            P("lat", None),
            P("lat", None),
            P("lat", None, None),
            P(),
            P(),
            P(),
            P(),
            P(),
        ),
        out_specs=P("member", "lat", "lon", None),
        check_vma=False,
    )
```

```python
import functools

import jax
import jax.numpy as jnp
from jax import lax
from jax.experimental import pallas as pl
from jax.experimental.pallas import tpu as pltpu
from jax.sharding import PartitionSpec as P

B = 3
HW = 8
PASSES = 2
K = 9
GROUP = 6


def ring_padded(cells, sides, width, closed):
    for axis, dim in sides:
        count = lax.axis_size(axis)
        ends = count if closed else count - 1
        head = lax.slice_in_dim(cells, 0, width, axis=dim)
        tail = lax.slice_in_dim(cells, cells.shape[dim] - width, cells.shape[dim], axis=dim)
        cells = jnp.concatenate(
            [
                lax.ppermute(tail, axis, [(i, (i + 1) % count) for i in range(ends)]),
                cells,
                lax.ppermute(head, axis, [((i + 1) % count, i) for i in range(ends)]),
            ],
            axis=dim,
        )
    return cells


def extend(state):
    count = lax.axis_size("lon")
    rows = ring_padded(state, (("lat", 0),), 1, False)
    edges = jnp.stack([state[0], state[-1]])
    flipped = lax.ppermute(edges, "lon", [(i, (i + count // 2) % count) for i in range(count)])
    band = lax.axis_index("lat")
    last_band = lax.axis_size("lat") - 1
    top = jnp.where(band == 0, flipped[0], rows[0])
    bottom = jnp.where(band == last_band, flipped[1], rows[-1])
    rows = jnp.concatenate([top[None], rows[1:-1], bottom[None]], axis=0)
    return ring_padded(rows, (("lon", 1),), HW, True)


def window_pass(state, lat_offsets, lon_offsets, psi, w_disco, norm_gain, w_up, bias_up, w_down):
    row_count, col_count, width = state.shape
    extended = extend(state)
    span = col_count + 2 * HW
    stacked = jnp.concatenate(
        [extended[0:row_count], extended[1 : row_count + 1], extended[2 : row_count + 2]], axis=1
    )
    row_pick = (
        (lat_offsets + 1)[:, :, None] == jnp.arange(3, dtype=jnp.int32)[None, None, :]
    ).astype(jnp.float32)
    target = jnp.arange(col_count, dtype=jnp.int32)[None, None, :] + HW + lon_offsets[:, :, None]
    col_pick = (
        target[:, :, :, None] == jnp.arange(span, dtype=jnp.int32)[None, None, None, :]
    ).astype(jnp.float32)
    weights = jnp.einsum(
        "ikb,ikr,ikjq->bijrq", psi, row_pick, col_pick, precision=lax.Precision.HIGHEST
    )
    weights = weights.reshape(B, row_count, col_count, 3 * span)
    mix = jnp.einsum(
        "bijp,ipc->bijc", weights, stacked.astype(jnp.float32), precision=lax.Precision.HIGHEST
    )
    mix = mix.astype(jnp.bfloat16)
    inner = state.astype(jnp.float32).reshape(-1, width)
    for basis in range(B):
        inner = inner + jnp.dot(
            mix[basis].reshape(-1, width), w_disco[basis], preferred_element_type=jnp.float32
        )
    mean = jnp.mean(inner, axis=1, keepdims=True)
    centred = inner - mean
    variance = jnp.mean(centred * centred, axis=1, keepdims=True)
    normed = (centred * lax.rsqrt(variance + 1e-05) * norm_gain).astype(jnp.bfloat16)
    hidden = jax.nn.gelu(
        jnp.dot(normed, w_up, preferred_element_type=jnp.float32) + bias_up
    ).astype(jnp.bfloat16)
    result = inner + jnp.dot(hidden, w_down, preferred_element_type=jnp.float32)
    return result.astype(jnp.bfloat16).reshape(row_count, col_count, width)


def window_shards(
    analysis, noise, w_in, lat_offsets, lon_offsets, psi, w_disco, norm_gain, w_up, bias_up, w_down
):
    row_count, col_count, quarter = analysis.shape
    width = w_in.shape[1]
    start = lax.axis_index("member") * quarter
    own_rows = lax.dynamic_slice_in_dim(w_in, start, quarter, 0)
    partial_base = jnp.dot(
        analysis.reshape(-1, quarter), own_rows, preferred_element_type=jnp.float32
    )
    base = lax.psum(partial_base.astype(jnp.bfloat16), "member").astype(jnp.float32)
    state = (base + noise[0].reshape(-1, width).astype(jnp.float32)).astype(jnp.bfloat16)
    state = state.reshape(row_count, col_count, width)
    for step in range(PASSES):
        state = window_pass(
            state, lat_offsets, lon_offsets, psi, w_disco, norm_gain, w_up, bias_up, w_down
        )
    return state[None]


def border_kernel(border_ref):
    border_ref[...] = jnp.zeros_like(border_ref)


def weights_kernel(
    lat_ref, lon_ref, psi_ref, w_in_ref, w_disco_ref, w_up_ref, w_down_ref, gain_ref, bias_ref,
    weights_ref, spread_ref, disco_out, up_out, down_out, gain_out, bias_out, in_ref, sems,
):
    pairs = (
        (w_in_ref, in_ref), (w_disco_ref, disco_out), (w_up_ref, up_out),
        (w_down_ref, down_out), (gain_ref, gain_out), (bias_ref, bias_out),
    )
    copies = [
        pltpu.make_async_copy(source, target, sems.at[i]) for i, (source, target) in enumerate(pairs)
    ]
    for copy in copies:
        copy.start()
    f32 = jnp.float32
    rows = lat_ref.shape[1]
    band = lax.axis_index("lat")
    row = lax.broadcasted_iota(jnp.int32, (K, rows), 1)
    up, along = lat_ref[...], lon_ref[...]
    crossing = ((band == 0) & (row == 0) & (up < 0)) | (
        (band == lax.axis_size("lat") - 1) & (row == rows - 1) & (up > 0)
    )
    place = jnp.where(crossing, 1, up + 1) * 16 + ((along + jnp.where(crossing, 8, 0)) & 15)
    spot = lax.broadcasted_iota(jnp.int32, (48, rows), 0)
    sums = [jnp.zeros((48, rows), f32) for _ in range(B)]
    for k in range(K):
        hit = spot == place[k : k + 1]
        for b in range(B):
            sums[b] = sums[b] + jnp.where(hit, psi_ref[k, b : b + 1, :], 0.0)
    lines = [
        jnp.transpose(jnp.pad(part, ((0, 80), (0, 128 - rows))))[:rows] for part in sums
    ]
    col = lax.broadcasted_iota(jnp.int32, (16, 128), 0)
    straight = lax.broadcasted_iota(jnp.int32, (16, 128), 1) % 16 >= col
    for i in range(rows):
        shift = (i + 1) % GROUP * 16
        for b in range(B):
            line = jnp.broadcast_to(lines[b][i : i + 1], (16, 128))
            turned = jnp.where(
                straight,
                pltpu.roll(line, shift, 1, stride=1, stride_axis=0),
                pltpu.roll(line, (shift + 112) % 128, 1, stride=1, stride_axis=0),
            )
            weights_ref[pl.ds((i * B + b) * 16, 16), :] = turned.astype(jnp.bfloat16)
    member = lax.axis_index("member")
    quarter = w_in_ref.shape[0] // 4
    copies[0].wait()
    even = member - member % 2
    groups = (
        member, member ^ 1, member ^ 2, member ^ 3, even, even ^ 1, even ^ 3, even ^ 2
    )
    for place, group in enumerate(groups):
        spread_ref[pl.ds(place * quarter, quarter), :] = in_ref[
            pl.ds(pl.multiple_of(group * quarter, quarter), quarter), :
        ]
    for copy in copies[1:]:
        copy.wait()


def start_kernel(
    chip_ref, x_ref, sent_ref, got_ref, noise_ref, from_y_ref, spread_ref, weights_ref, border_ref,
    state_ref, first_ref, second_ref,
):
    f32, bf16 = jnp.float32, jnp.bfloat16
    rows, cols, width = noise_ref.shape
    wide = lambda block: block.astype(f32).reshape(rows * cols, block.shape[2])
    sent, got = wide(sent_ref[...]), wide(got_ref[...])
    even_core = lax.axis_index("member") % 2 == 0
    along_y, diagonal = jnp.where(even_core, sent, got), jnp.where(even_core, got, sent)

    def base_of(parts, first):
        analysis = jnp.concatenate(parts, axis=1).astype(bf16)
        base = jnp.dot(
            analysis, spread_ref[pl.ds(first, analysis.shape[1]), :], preferred_element_type=f32
        )
        return base.reshape(rows, cols, width)

    own = base_of([wide(chip_ref[pl.ds(0, rows)]), wide(x_ref[pl.ds(0, rows)])], 0)
    other = base_of([along_y, diagonal], width)
    state = jnp.concatenate(
        [own + noise_ref[...].astype(f32), other + from_y_ref[...].astype(f32)], axis=1
    )
    state = state.astype(bf16).reshape(rows * 16, width)
    state_ref[pl.ds(0, 32), :] = border_ref[...]
    state_ref[pl.ds(32, rows * 16), :] = state
    state_ref[pl.ds(32 + rows * 16, 32), :] = border_ref[...]
    even = lax.axis_index("lat") % 2 == 0
    for ref, last in ((first_ref, even), (second_ref, jnp.logical_not(even))):
        line = pl.multiple_of(jnp.where(last, (rows - 1) * B * 16, 0), 16)
        cell = pl.multiple_of(jnp.where(last, rows * 16, 32), 16)
        ref[pl.ds(0, 32), :] = state_ref[pl.ds(cell, 32), pl.ds(0, 128)]
        ref[pl.ds(32, 32), :] = state_ref[pl.ds(cell, 32), pl.ds(128, 128)]
        ref[pl.ds(64, B * 16), :] = weights_ref[pl.ds(line, B * 16), :]


def mixed(weights, state, count, width):
    mix = jnp.dot(weights, state, preferred_element_type=jnp.float32)
    return mix.reshape(count, B, 16, width)


def cell_block(
    before, mix, w_disco_ref, gain_ref, w_up_ref, bias_ref, w_down_ref, gain_up=None, norm_first=True
):
    f32, bf16 = jnp.float32, jnp.bfloat16
    count, width = before.shape
    inner = before + jnp.dot(
        mix, w_disco_ref[...].reshape(B * width, width), preferred_element_type=f32
    )
    mean = jnp.mean(inner, axis=1, keepdims=True)
    variance = jnp.mean(inner * inner, axis=1, keepdims=True) - mean * mean
    scale = lax.rsqrt(jnp.maximum(variance, 0.0) + 1e-05)
    if gain_up is None:
        gain = jnp.broadcast_to(gain_ref[...], (16, width))
        rounded = gain.astype(bf16).astype(f32)
        row = lax.broadcasted_iota(jnp.int32, gain.shape, 0)
        parts = jnp.where(row == 0, rounded, jnp.where(row == 1, gain - rounded, 0.0))
        normed = (inner - mean) * scale * gain_ref[...]
        up = jnp.dot(
            jnp.concatenate([normed.astype(bf16), parts.astype(bf16)], axis=0),
            w_up_ref[...],
            preferred_element_type=f32,
        )
        gain_up = up[count : count + 1] + up[count + 1 : count + 2]
        up = up[:count]
    elif norm_first:
        normed = (inner - mean) * scale * gain_ref[...]
        up = jnp.dot(normed.astype(bf16), w_up_ref[...], preferred_element_type=f32)
    else:
        scaled = (inner * gain_ref[...]).astype(bf16)
        up = jnp.dot(scaled, w_up_ref[...], preferred_element_type=f32)
        up = (up - mean * gain_up) * scale
    hidden = jax.nn.gelu(up + bias_ref[...]).astype(bf16)
    return inner + jnp.dot(hidden, w_down_ref[...], preferred_element_type=f32), gain_up


def mixed_rows(low, high, rows, weights_ref, state_ref):
    first = low - low % GROUP
    reach = min(GROUP + 2, rows + 4 - first) * 16
    return mixed(
        weights_ref[pl.ds((low - 1) * B * 16, (high - low) * B * 16), pl.ds(0, reach)],
        state_ref[pl.ds(first * 16, reach), :],
        high - low,
        state_ref.shape[1],
    )


def inner_kernel(
    state_ref, weights_ref, w_disco_ref, gain_ref, w_up_ref, bias_ref, w_down_ref,
    near_ref, out_ref, gain_up_ref, next_ref, mix_ref, own_mix_ref,
):
    f32, bf16 = jnp.float32, jnp.bfloat16
    width = state_ref.shape[1]
    rows, cols = out_ref.shape[0] + 4, out_ref.shape[1]
    block = functools.partial(
        cell_block, w_disco_ref=w_disco_ref, gain_ref=gain_ref, w_up_ref=w_up_ref,
        bias_ref=bias_ref, w_down_ref=w_down_ref,
    )
    for first in range(0, rows, GROUP):
        low, high = max(first, 2), min(first + GROUP, rows)
        mix = mixed_rows(low, high, rows, weights_ref, state_ref)
        for i in range(low, high):
            for b in range(B):
                mix_ref[pl.ds((i - 2) * 16, 16), pl.ds(b * width, width)] = mix[i - low, b].astype(bf16)
    after, gain_up = block(
        state_ref[pl.ds(48, (rows - 2) * 16), :].astype(f32), mix_ref[...]
    )
    after = after.astype(bf16)
    gain_up_ref[...] = gain_up
    border = jnp.zeros((48, width), bf16)
    next_ref[pl.ds(0, 48), :] = border
    next_ref[pl.ds(48, (rows - 2) * 16), :] = after
    next_ref[pl.ds(16 + rows * 16, 48), :] = border
    near_ref[pl.ds(0, 32), :] = after[:32]
    near_ref[pl.ds(32, 32), :] = after[(rows - 4) * 16 :]
    for first in range(0, rows - 1, GROUP):
        low, high = max(first, 3), min(first + GROUP, rows - 1)
        mix = mixed_rows(low, high, rows, weights_ref, next_ref)
        for i in range(low, high):
            for b in range(B):
                own_mix_ref[pl.ds((i - 3) * cols, cols), pl.ds(b * width, width)] = mix[i - low, b, :cols]
    own = next_ref[pl.ds(64, (rows - 4) * 16), :].astype(f32).reshape(rows - 4, 16, width)[:, :cols]
    result, _ = block(
        own.reshape((rows - 4) * cols, width), own_mix_ref[...].astype(bf16), gain_up=gain_up
    )
    out_ref[...] = result.reshape(rows - 4, cols, width).astype(bf16)


def edge_kernel(
    state_ref, near_ref, inner_ref, first_ref, second_ref, weights_ref,
    w_disco_ref, gain_ref, w_up_ref, bias_ref, w_down_ref, gain_up_ref, out_ref, next_ref, last_ref, sems,
):
    f32, bf16 = jnp.float32, jnp.bfloat16
    rows, cols, width = out_ref.shape
    block = functools.partial(
        cell_block, w_disco_ref=w_disco_ref, gain_ref=gain_ref, w_up_ref=w_up_ref,
        bias_ref=bias_ref, w_down_ref=w_down_ref, gain_up=gain_up_ref[...],
        norm_first=False,
    )
    inner_copy = pltpu.make_async_copy(inner_ref, out_ref.at[pl.ds(2, rows - 4)], sems.at[0])
    inner_copy.start()
    line = B * 16
    even = lax.axis_index("lat") % 2 == 0
    first, second = first_ref[...], second_ref[...]
    top, bottom = jnp.where(even, second, first), jnp.where(even, first, second)

    def received(side):
        return jnp.concatenate([side[:32], side[32:64]], axis=1)

    def one_row(mix):
        return jnp.concatenate([mix[b] for b in range(B)], axis=1)

    top_state = jnp.concatenate([received(top), state_ref[pl.ds(32, 32), :]], axis=0)
    top_mix = mixed(
        jnp.concatenate([top[64:], weights_ref[pl.ds(0, line), :]], axis=0)[:, :64],
        top_state, 2, width,
    )
    bottom_state = jnp.concatenate(
        [state_ref[pl.ds(rows * 16, 32), :], received(bottom)], axis=0
    )
    bottom_mix = mixed(
        jnp.concatenate(
            [weights_ref[pl.ds((rows - 1) * line, line), :], bottom[64:]], axis=0
        )[:, :64],
        bottom_state, 2, width,
    )
    edge_mix = jnp.concatenate(
        [one_row(mix[i]) for mix in (top_mix, bottom_mix) for i in range(2)], axis=0
    ).astype(bf16)
    edge_state = jnp.concatenate([top_state[16:48], bottom_state[16:48]], axis=0)
    edge = block(edge_state.astype(f32), edge_mix)[0].astype(bf16)
    next_ref[...] = jnp.zeros_like(next_ref)
    next_ref[pl.ds(16, 32), :] = edge[:32]
    next_ref[pl.ds(48, 32), :] = near_ref[pl.ds(0, 32), :]
    next_ref[pl.ds((rows - 1) * 16, 32), :] = near_ref[pl.ds(32, 32), :]
    next_ref[pl.ds((rows + 1) * 16, 32), :] = edge[32:]
    mixes, own = [], []
    for low, high in ((1, 3), (rows - 1, rows), (rows, rows + 1)):
        mix = mixed_rows(low, high, rows, weights_ref, next_ref)
        for i in range(low, high):
            mixes.append(one_row(mix[i - low, :, :cols]))
            own.append(next_ref[pl.ds((i + 1) * 16, 16), :].astype(f32)[:cols])
    result, _ = block(jnp.concatenate(own, axis=0), jnp.concatenate(mixes, axis=0).astype(bf16))
    last_ref[...] = result.reshape(4, cols, width).astype(bf16)
    top_copy = pltpu.make_async_copy(
        last_ref.at[pl.ds(0, 2)], out_ref.at[pl.ds(0, 2)], sems.at[1]
    )
    bottom_copy = pltpu.make_async_copy(
        last_ref.at[pl.ds(2, 2)], out_ref.at[pl.ds(rows - 2, 2)], sems.at[2]
    )
    top_copy.start()
    bottom_copy.start()
    inner_copy.wait()
    top_copy.wait()
    bottom_copy.wait()


def circle_shards(
    analysis, noise, w_in, lat_offsets, lon_offsets, psi, w_disco, norm_gain, w_up, bias_up, w_down
):
    f32, bf16 = jnp.float32, jnp.bfloat16
    rows, cols, quarter = analysis.shape
    width = w_in.shape[1]
    noise = noise[0]
    bands = lax.axis_size("lat")
    members = lax.axis_size("member")
    line = B * 16
    vmem = pl.BlockSpec(memory_space=pltpu.VMEM)
    hbm = pl.BlockSpec(memory_space=pltpu.HBM)
    params = pltpu.CompilerParams(vmem_limit_bytes=12 * 1024 * 1024)

    def shape(*dims, dtype=bf16):
        return jax.ShapeDtypeStruct(dims, dtype)

    def swapped(block, partner):
        pairs = [(i, partner(i)) for i in range(2 * members)]
        return lax.ppermute(block, ("member", "lon"), pairs)

    from_y = swapped(noise, lambda i: i ^ 1)
    from_core = swapped(analysis, lambda i: i ^ 2)
    border = pl.pallas_call(
        border_kernel,
        out_shape=shape(32, width),
        out_specs=vmem,
        cost_estimate=pl.CostEstimate(flops=1_000_000_000, bytes_accessed=16_384, transcendentals=0),
        compiler_params=params,
    )()
    analysis, border = lax.optimization_barrier((analysis, border))
    chip = jnp.pad(jnp.concatenate([analysis, from_core], axis=2), ((0, 1), (0, 0), (0, 0)))
    across = swapped(chip, lambda i: i ^ 5 if i & 2 else i ^ 1)
    from_x = swapped(chip, lambda i: i ^ 4)
    weights, spread, *dense = pl.pallas_call(
        weights_kernel,
        out_shape=(
            shape(rows * line, 128), shape(8 * quarter, width), shape(*w_disco.shape),
            shape(*w_up.shape), shape(*w_down.shape), shape(1, width, dtype=f32),
            shape(1, w_up.shape[1], dtype=f32),
        ),
        in_specs=[vmem] * 3 + [hbm] * 6,
        out_specs=(vmem,) * 7,
        scratch_shapes=[pltpu.VMEM(w_in.shape, bf16), pltpu.SemaphoreType.DMA((6,))],
        cost_estimate=pl.CostEstimate(flops=4_000, bytes_accessed=3_000, transcendentals=0),
        compiler_params=params,
    )(
        lat_offsets.T,
        lon_offsets.T,
        jnp.transpose(psi, (1, 2, 0)),
        *(
            pltpu.with_memory_space_constraint(w, pltpu.HBM)
            for w in (
                w_in, w_disco, w_up, w_down, norm_gain.reshape(1, -1), bias_up.reshape(1, -1)
            )
        ),
    )
    w_disco, w_up, w_down, norm_gain, bias_up = dense
    dense = (w_disco, norm_gain, w_up, bias_up, w_down)

    across, from_y, weights = lax.optimization_barrier((across, from_y, weights))
    across = across[:rows]
    got = swapped(across, lambda i: i ^ 2)
    state, first, second = pl.pallas_call(
        start_kernel,
        out_shape=(shape((rows + 4) * 16, width), shape(64 + line, 128), shape(64 + line, 128)),
        in_specs=[vmem] * 9,
        out_specs=(vmem,) * 3,
        cost_estimate=pl.CostEstimate(flops=200_000_000, bytes_accessed=1_000_000, transcendentals=0),
        compiler_params=params,
    )(chip, from_x, across, got, noise, from_y, spread, weights, border)
    def paired(edge, start):
        pairs = []
        for i in range(members):
            for j in range(bands):
                k = j + 1 if (j - start) % 2 == 0 else j - 1
                there = (i, k) if min(j, k) >= start and k < bands else (i ^ 1, j)
                pairs.append((i * bands + j, there[0] * bands + there[1]))
        return lax.ppermute(edge, ("member", "lat"), pairs)

    first, second = paired(first, 0), paired(second, 1)
    near, inner, gain_up = pl.pallas_call(
        inner_kernel,
        out_shape=(
            shape(64, width), shape(rows - 4, cols, width), shape(1, w_up.shape[1], dtype=f32)
        ),
        in_specs=[vmem] * 7,
        out_specs=(vmem,) * 3,
        scratch_shapes=[
            pltpu.VMEM(((rows + 4) * 16, width), bf16),
            pltpu.VMEM(((rows - 2) * 16, B * width), bf16),
            pltpu.VMEM(((rows - 4) * cols, B * width), f32),
        ],
        cost_estimate=pl.CostEstimate(
            flops=800_000_000, bytes_accessed=2_000_000, transcendentals=400_000
        ),
        compiler_params=params,
    )(state, weights, *dense)
    result = pl.pallas_call(
        edge_kernel,
        out_shape=shape(rows, cols, width),
        in_specs=[vmem] * 12,
        out_specs=pl.BlockSpec(memory_space=pl.ANY),
        scratch_shapes=[
            pltpu.VMEM(((rows + 4) * 16, width), bf16),
            pltpu.VMEM((4, cols, width), bf16),
            pltpu.SemaphoreType.DMA((3,)),
        ],
        cost_estimate=pl.CostEstimate(
            flops=100_000_000, bytes_accessed=2_000_000, transcendentals=50_000
        ),
        compiler_params=params,
    )(state, near, inner, first, second, weights, *dense, gain_up)
    return result[None]


def solution(mesh):
    circle = mesh.shape["lon"] == 2 and mesh.shape["member"] == 4
    return jax.shard_map(
        circle_shards if circle else window_shards,
        mesh=mesh,
        in_specs=(
            P("lat", "lon", "member"),
            P("member", "lat", "lon", None),
            P(),
            P("lat", None),
            P("lat", None),
            P("lat", None, None),
            P(),
            P(),
            P(),
            P(),
            P(),
        ),
        out_specs=P("member", "lat", "lon", None),
        check_vma=False,
    )
```

```python
import functools

import jax
import jax.numpy as jnp
from jax import lax
from jax.experimental import pallas as pl
from jax.experimental.pallas import tpu as pltpu
from jax.sharding import PartitionSpec as P

B = 3
HW = 8
PASSES = 2
K = 9
GROUP = 6


def ring_padded(cells, sides, width, closed):
    for axis, dim in sides:
        count = lax.axis_size(axis)
        ends = count if closed else count - 1
        head = lax.slice_in_dim(cells, 0, width, axis=dim)
        tail = lax.slice_in_dim(cells, cells.shape[dim] - width, cells.shape[dim], axis=dim)
        cells = jnp.concatenate(
            [
                lax.ppermute(tail, axis, [(i, (i + 1) % count) for i in range(ends)]),
                cells,
                lax.ppermute(head, axis, [((i + 1) % count, i) for i in range(ends)]),
            ],
            axis=dim,
        )
    return cells


def extend(state):
    count = lax.axis_size("lon")
    rows = ring_padded(state, (("lat", 0),), 1, False)
    edges = jnp.stack([state[0], state[-1]])
    flipped = lax.ppermute(edges, "lon", [(i, (i + count // 2) % count) for i in range(count)])
    band = lax.axis_index("lat")
    last_band = lax.axis_size("lat") - 1
    top = jnp.where(band == 0, flipped[0], rows[0])
    bottom = jnp.where(band == last_band, flipped[1], rows[-1])
    rows = jnp.concatenate([top[None], rows[1:-1], bottom[None]], axis=0)
    return ring_padded(rows, (("lon", 1),), HW, True)


def window_pass(state, lat_offsets, lon_offsets, psi, w_disco, norm_gain, w_up, bias_up, w_down):
    row_count, col_count, width = state.shape
    extended = extend(state)
    span = col_count + 2 * HW
    stacked = jnp.concatenate(
        [extended[0:row_count], extended[1 : row_count + 1], extended[2 : row_count + 2]], axis=1
    )
    row_pick = (
        (lat_offsets + 1)[:, :, None] == jnp.arange(3, dtype=jnp.int32)[None, None, :]
    ).astype(jnp.float32)
    target = jnp.arange(col_count, dtype=jnp.int32)[None, None, :] + HW + lon_offsets[:, :, None]
    col_pick = (
        target[:, :, :, None] == jnp.arange(span, dtype=jnp.int32)[None, None, None, :]
    ).astype(jnp.float32)
    weights = jnp.einsum(
        "ikb,ikr,ikjq->bijrq", psi, row_pick, col_pick, precision=lax.Precision.HIGHEST
    )
    weights = weights.reshape(B, row_count, col_count, 3 * span)
    mix = jnp.einsum(
        "bijp,ipc->bijc", weights, stacked.astype(jnp.float32), precision=lax.Precision.HIGHEST
    )
    mix = mix.astype(jnp.bfloat16)
    inner = state.astype(jnp.float32).reshape(-1, width)
    for basis in range(B):
        inner = inner + jnp.dot(
            mix[basis].reshape(-1, width), w_disco[basis], preferred_element_type=jnp.float32
        )
    mean = jnp.mean(inner, axis=1, keepdims=True)
    centred = inner - mean
    variance = jnp.mean(centred * centred, axis=1, keepdims=True)
    normed = (centred * lax.rsqrt(variance + 1e-05) * norm_gain).astype(jnp.bfloat16)
    hidden = jax.nn.gelu(
        jnp.dot(normed, w_up, preferred_element_type=jnp.float32) + bias_up
    ).astype(jnp.bfloat16)
    result = inner + jnp.dot(hidden, w_down, preferred_element_type=jnp.float32)
    return result.astype(jnp.bfloat16).reshape(row_count, col_count, width)


def window_shards(
    analysis, noise, w_in, lat_offsets, lon_offsets, psi, w_disco, norm_gain, w_up, bias_up, w_down
):
    row_count, col_count, quarter = analysis.shape
    width = w_in.shape[1]
    start = lax.axis_index("member") * quarter
    own_rows = lax.dynamic_slice_in_dim(w_in, start, quarter, 0)
    partial_base = jnp.dot(
        analysis.reshape(-1, quarter), own_rows, preferred_element_type=jnp.float32
    )
    base = lax.psum(partial_base.astype(jnp.bfloat16), "member").astype(jnp.float32)
    state = (base + noise[0].reshape(-1, width).astype(jnp.float32)).astype(jnp.bfloat16)
    state = state.reshape(row_count, col_count, width)
    for step in range(PASSES):
        state = window_pass(
            state, lat_offsets, lon_offsets, psi, w_disco, norm_gain, w_up, bias_up, w_down
        )
    return state[None]


def border_kernel(border_ref):
    border_ref[...] = jnp.zeros_like(border_ref)


def weights_kernel(
    lat_ref, lon_ref, psi_ref, w_in_ref, w_disco_ref, w_up_ref, w_down_ref, gain_ref, bias_ref,
    weights_ref, spread_ref, disco_out, up_out, down_out, gain_out, bias_out, in_ref, sems,
):
    pairs = (
        (w_in_ref, in_ref), (w_disco_ref, disco_out), (w_up_ref, up_out),
        (w_down_ref, down_out), (gain_ref, gain_out), (bias_ref, bias_out),
    )
    copies = [
        pltpu.make_async_copy(source, target, sems.at[i]) for i, (source, target) in enumerate(pairs)
    ]
    for copy in copies:
        copy.start()
    f32 = jnp.float32
    rows = lat_ref.shape[1]
    band = lax.axis_index("lat")
    row = lax.broadcasted_iota(jnp.int32, (K, rows), 1)
    up, along = lat_ref[...], lon_ref[...]
    crossing = ((band == 0) & (row == 0) & (up < 0)) | (
        (band == lax.axis_size("lat") - 1) & (row == rows - 1) & (up > 0)
    )
    place = jnp.where(crossing, 1, up + 1) * 16 + ((along + jnp.where(crossing, 8, 0)) & 15)
    spot = lax.broadcasted_iota(jnp.int32, (48, rows), 0)
    sums = [jnp.zeros((48, rows), f32) for _ in range(B)]
    for k in range(K):
        hit = spot == place[k : k + 1]
        for b in range(B):
            sums[b] = sums[b] + jnp.where(hit, psi_ref[k, b : b + 1, :], 0.0)
    lines = [
        jnp.transpose(jnp.pad(part, ((0, 80), (0, 128 - rows))))[:rows] for part in sums
    ]
    col = lax.broadcasted_iota(jnp.int32, (16, 128), 0)
    straight = lax.broadcasted_iota(jnp.int32, (16, 128), 1) % 16 >= col
    for i in range(rows):
        shift = (i + 1) % GROUP * 16
        for b in range(B):
            line = jnp.broadcast_to(lines[b][i : i + 1], (16, 128))
            turned = jnp.where(
                straight,
                pltpu.roll(line, shift, 1, stride=1, stride_axis=0),
                pltpu.roll(line, (shift + 112) % 128, 1, stride=1, stride_axis=0),
            )
            weights_ref[pl.ds((i * B + b) * 16, 16), :] = turned.astype(jnp.bfloat16)
    member = lax.axis_index("member")
    quarter = w_in_ref.shape[0] // 4
    copies[0].wait()
    even = member - member % 2
    groups = (
        member, member ^ 1, member ^ 2, member ^ 3, even, even ^ 1, even ^ 3, even ^ 2
    )
    for place, group in enumerate(groups):
        spread_ref[pl.ds(place * quarter, quarter), :] = in_ref[
            pl.ds(pl.multiple_of(group * quarter, quarter), quarter), :
        ]
    for copy in copies[1:]:
        copy.wait()


def start_kernel(
    chip_ref, x_ref, sent_ref, got_ref, noise_ref, from_y_ref, spread_ref, weights_ref, border_ref,
    state_ref, first_ref, second_ref,
):
    f32, bf16 = jnp.float32, jnp.bfloat16
    rows, cols, width = noise_ref.shape
    wide = lambda block: block.astype(f32).reshape(rows * cols, block.shape[2])
    sent, got = wide(sent_ref[...]), wide(got_ref[...])
    even_core = lax.axis_index("member") % 2 == 0
    along_y, diagonal = jnp.where(even_core, sent, got), jnp.where(even_core, got, sent)

    def base_of(parts, first):
        analysis = jnp.concatenate(parts, axis=1).astype(bf16)
        base = jnp.dot(
            analysis, spread_ref[pl.ds(first, analysis.shape[1]), :], preferred_element_type=f32
        )
        return base.reshape(rows, cols, width)

    own = base_of([wide(chip_ref[pl.ds(0, rows)]), wide(x_ref[pl.ds(0, rows)])], 0)
    other = base_of([along_y, diagonal], width)
    state = jnp.concatenate(
        [own + noise_ref[...].astype(f32), other + from_y_ref[...].astype(f32)], axis=1
    )
    state = state.astype(bf16).reshape(rows * 16, width)
    state_ref[pl.ds(0, 32), :] = border_ref[...]
    state_ref[pl.ds(32, rows * 16), :] = state
    state_ref[pl.ds(32 + rows * 16, 32), :] = border_ref[...]
    even = lax.axis_index("lat") % 2 == 0
    for ref, last in ((first_ref, even), (second_ref, jnp.logical_not(even))):
        line = pl.multiple_of(jnp.where(last, (rows - 1) * B * 16, 0), 16)
        cell = pl.multiple_of(jnp.where(last, rows * 16, 32), 16)
        ref[pl.ds(0, 32), :] = state_ref[pl.ds(cell, 32), pl.ds(0, 128)]
        ref[pl.ds(32, 32), :] = state_ref[pl.ds(cell, 32), pl.ds(128, 128)]
        ref[pl.ds(64, B * 16), :] = weights_ref[pl.ds(line, B * 16), :]


def mixed(weights, state, count, width):
    mix = jnp.dot(weights, state, preferred_element_type=jnp.float32)
    return mix.reshape(count, B, 16, width)


def cell_block(
    before, mix, w_disco_ref, gain_ref, w_up_ref, bias_ref, w_down_ref, gain_up=None, norm_first=True
):
    f32, bf16 = jnp.float32, jnp.bfloat16
    count, width = before.shape
    inner = before + jnp.dot(
        mix, w_disco_ref[...].reshape(B * width, width), preferred_element_type=f32
    )
    mean = jnp.mean(inner, axis=1, keepdims=True)
    variance = jnp.mean(inner * inner, axis=1, keepdims=True) - mean * mean
    scale = lax.rsqrt(jnp.maximum(variance, 0.0) + 1e-05)
    if gain_up is None:
        gain = jnp.broadcast_to(gain_ref[...], (16, width))
        rounded = gain.astype(bf16).astype(f32)
        row = lax.broadcasted_iota(jnp.int32, gain.shape, 0)
        parts = jnp.where(row == 0, rounded, jnp.where(row == 1, gain - rounded, 0.0))
        normed = (inner - mean) * scale * gain_ref[...]
        up = jnp.dot(
            jnp.concatenate([normed.astype(bf16), parts.astype(bf16)], axis=0),
            w_up_ref[...],
            preferred_element_type=f32,
        )
        gain_up = up[count : count + 1] + up[count + 1 : count + 2]
        up = up[:count]
    elif norm_first:
        normed = (inner - mean) * scale * gain_ref[...]
        up = jnp.dot(normed.astype(bf16), w_up_ref[...], preferred_element_type=f32)
    else:
        scaled = (inner * gain_ref[...]).astype(bf16)
        up = jnp.dot(scaled, w_up_ref[...], preferred_element_type=f32)
        up = (up - mean * gain_up) * scale
    hidden = jax.nn.gelu(up + bias_ref[...]).astype(bf16)
    return inner + jnp.dot(hidden, w_down_ref[...], preferred_element_type=f32), gain_up


def mixed_rows(low, high, rows, weights_ref, state_ref):
    first = low - low % GROUP
    reach = min(GROUP + 2, rows + 4 - first) * 16
    return mixed(
        weights_ref[pl.ds((low - 1) * B * 16, (high - low) * B * 16), pl.ds(0, reach)],
        state_ref[pl.ds(first * 16, reach), :],
        high - low,
        state_ref.shape[1],
    )


def inner_kernel(
    state_ref, weights_ref, w_disco_ref, gain_ref, w_up_ref, bias_ref, w_down_ref,
    near_ref, out_ref, gain_up_ref, next_ref, mix_ref, own_mix_ref,
):
    f32, bf16 = jnp.float32, jnp.bfloat16
    width = state_ref.shape[1]
    rows, cols = out_ref.shape[0] + 4, out_ref.shape[1]
    block = functools.partial(
        cell_block, w_disco_ref=w_disco_ref, gain_ref=gain_ref, w_up_ref=w_up_ref,
        bias_ref=bias_ref, w_down_ref=w_down_ref,
    )
    for first in range(0, rows, GROUP):
        low, high = max(first, 2), min(first + GROUP, rows)
        mix = mixed_rows(low, high, rows, weights_ref, state_ref)
        for i in range(low, high):
            for b in range(B):
                mix_ref[pl.ds((i - 2) * 16, 16), pl.ds(b * width, width)] = mix[i - low, b].astype(bf16)
    after, gain_up = block(
        state_ref[pl.ds(48, (rows - 2) * 16), :].astype(f32), mix_ref[...]
    )
    after = after.astype(bf16)
    gain_up_ref[...] = gain_up
    border = jnp.zeros((48, width), bf16)
    next_ref[pl.ds(0, 48), :] = border
    next_ref[pl.ds(48, (rows - 2) * 16), :] = after
    next_ref[pl.ds(16 + rows * 16, 48), :] = border
    near_ref[pl.ds(0, 32), :] = after[:32]
    near_ref[pl.ds(32, 32), :] = after[(rows - 4) * 16 :]
    for first in range(0, rows - 1, GROUP):
        low, high = max(first, 3), min(first + GROUP, rows - 1)
        mix = mixed_rows(low, high, rows, weights_ref, next_ref)
        for i in range(low, high):
            for b in range(B):
                own_mix_ref[pl.ds((i - 3) * cols, cols), pl.ds(b * width, width)] = mix[i - low, b, :cols]
    own = next_ref[pl.ds(64, (rows - 4) * 16), :].astype(f32).reshape(rows - 4, 16, width)[:, :cols]
    result, _ = block(
        own.reshape((rows - 4) * cols, width), own_mix_ref[...].astype(bf16), gain_up=gain_up
    )
    out_ref[...] = result.reshape(rows - 4, cols, width).astype(bf16)


def edge_kernel(
    state_ref, near_ref, inner_ref, first_ref, second_ref, weights_ref,
    w_disco_ref, gain_ref, w_up_ref, bias_ref, w_down_ref, gain_up_ref, out_ref, next_ref, last_ref, sems,
):
    f32, bf16 = jnp.float32, jnp.bfloat16
    rows, cols, width = out_ref.shape
    block = functools.partial(
        cell_block, w_disco_ref=w_disco_ref, gain_ref=gain_ref, w_up_ref=w_up_ref,
        bias_ref=bias_ref, w_down_ref=w_down_ref, gain_up=gain_up_ref[...],
        norm_first=False,
    )
    inner_copy = pltpu.make_async_copy(inner_ref, out_ref.at[pl.ds(2, rows - 4)], sems.at[0])
    inner_copy.start()
    for start, count in ((0, 16), (80, 48), ((rows - 6) * 16, 80), ((rows + 3) * 16, 16)):
        next_ref[pl.ds(start, count), :] = jnp.zeros((count, width), bf16)
    next_ref[pl.ds(48, 32), :] = near_ref[pl.ds(0, 32), :]
    next_ref[pl.ds((rows - 1) * 16, 32), :] = near_ref[pl.ds(32, 32), :]
    line = B * 16
    even = lax.axis_index("lat") % 2 == 0
    first, second = first_ref[...], second_ref[...]
    top, bottom = jnp.where(even, second, first), jnp.where(even, first, second)

    def received(side):
        return jnp.concatenate([side[:32], side[32:64]], axis=1)

    def one_row(mix):
        return jnp.concatenate([mix[b] for b in range(B)], axis=1)

    top_state = jnp.concatenate([received(top), state_ref[pl.ds(32, 32), :]], axis=0)
    top_mix = mixed(
        jnp.concatenate([top[64:], weights_ref[pl.ds(0, line), :]], axis=0)[:, :64],
        top_state, 2, width,
    )
    bottom_state = jnp.concatenate(
        [state_ref[pl.ds(rows * 16, 32), :], received(bottom)], axis=0
    )
    bottom_mix = mixed(
        jnp.concatenate(
            [weights_ref[pl.ds((rows - 1) * line, line), :], bottom[64:]], axis=0
        )[:, :64],
        bottom_state, 2, width,
    )
    edge_mix = jnp.concatenate(
        [one_row(mix[i]) for mix in (top_mix, bottom_mix) for i in range(2)], axis=0
    ).astype(bf16)
    edge_state = jnp.concatenate([top_state[16:48], bottom_state[16:48]], axis=0)
    edge = block(edge_state.astype(f32), edge_mix)[0].astype(bf16)
    next_ref[pl.ds(16, 32), :] = edge[:32]
    next_ref[pl.ds((rows + 1) * 16, 32), :] = edge[32:]
    mixes, own = [], []
    for low, high in ((1, 3), (rows - 1, rows), (rows, rows + 1)):
        mix = mixed_rows(low, high, rows, weights_ref, next_ref)
        for i in range(low, high):
            mixes.append(one_row(mix[i - low, :, :cols]))
            own.append(next_ref[pl.ds((i + 1) * 16, 16), :].astype(f32)[:cols])
    result, _ = block(jnp.concatenate(own, axis=0), jnp.concatenate(mixes, axis=0).astype(bf16))
    last_ref[...] = result.reshape(4, cols, width).astype(bf16)
    top_copy = pltpu.make_async_copy(
        last_ref.at[pl.ds(0, 2)], out_ref.at[pl.ds(0, 2)], sems.at[1]
    )
    bottom_copy = pltpu.make_async_copy(
        last_ref.at[pl.ds(2, 2)], out_ref.at[pl.ds(rows - 2, 2)], sems.at[2]
    )
    top_copy.start()
    bottom_copy.start()
    inner_copy.wait()
    top_copy.wait()
    bottom_copy.wait()


def circle_shards(
    analysis, noise, w_in, lat_offsets, lon_offsets, psi, w_disco, norm_gain, w_up, bias_up, w_down
):
    f32, bf16 = jnp.float32, jnp.bfloat16
    rows, cols, quarter = analysis.shape
    width = w_in.shape[1]
    noise = noise[0]
    bands = lax.axis_size("lat")
    members = lax.axis_size("member")
    line = B * 16
    vmem = pl.BlockSpec(memory_space=pltpu.VMEM)
    hbm = pl.BlockSpec(memory_space=pltpu.HBM)
    params = pltpu.CompilerParams(vmem_limit_bytes=12 * 1024 * 1024)

    def shape(*dims, dtype=bf16):
        return jax.ShapeDtypeStruct(dims, dtype)

    def swapped(block, partner):
        pairs = [(i, partner(i)) for i in range(2 * members)]
        return lax.ppermute(block, ("member", "lon"), pairs)

    from_y = swapped(noise, lambda i: i ^ 1)
    from_core = swapped(analysis, lambda i: i ^ 2)
    border = pl.pallas_call(
        border_kernel,
        out_shape=shape(32, width),
        out_specs=vmem,
        cost_estimate=pl.CostEstimate(flops=1_000_000_000, bytes_accessed=16_384, transcendentals=0),
        compiler_params=params,
    )()
    analysis, border = lax.optimization_barrier((analysis, border))
    chip = jnp.pad(jnp.concatenate([analysis, from_core], axis=2), ((0, 1), (0, 0), (0, 0)))
    across = swapped(chip, lambda i: i ^ 5 if i & 2 else i ^ 1)
    from_x = swapped(chip, lambda i: i ^ 4)
    weights, spread, *dense = pl.pallas_call(
        weights_kernel,
        out_shape=(
            shape(rows * line, 128), shape(8 * quarter, width), shape(*w_disco.shape),
            shape(*w_up.shape), shape(*w_down.shape), shape(1, width, dtype=f32),
            shape(1, w_up.shape[1], dtype=f32),
        ),
        in_specs=[vmem] * 3 + [hbm] * 6,
        out_specs=(vmem,) * 7,
        scratch_shapes=[pltpu.VMEM(w_in.shape, bf16), pltpu.SemaphoreType.DMA((6,))],
        cost_estimate=pl.CostEstimate(flops=4_000, bytes_accessed=3_000, transcendentals=0),
        compiler_params=params,
    )(
        lat_offsets.T,
        lon_offsets.T,
        jnp.transpose(psi, (1, 2, 0)),
        *(
            pltpu.with_memory_space_constraint(w, pltpu.HBM)
            for w in (
                w_in, w_disco, w_up, w_down, norm_gain.reshape(1, -1), bias_up.reshape(1, -1)
            )
        ),
    )
    w_disco, w_up, w_down, norm_gain, bias_up = dense
    dense = (w_disco, norm_gain, w_up, bias_up, w_down)

    across, from_y, weights = lax.optimization_barrier((across, from_y, weights))
    across = across[:rows]
    got = swapped(across, lambda i: i ^ 2)
    state, first, second = pl.pallas_call(
        start_kernel,
        out_shape=(shape((rows + 4) * 16, width), shape(64 + line, 128), shape(64 + line, 128)),
        in_specs=[vmem] * 9,
        out_specs=(vmem,) * 3,
        cost_estimate=pl.CostEstimate(flops=200_000_000, bytes_accessed=1_000_000, transcendentals=0),
        compiler_params=params,
    )(chip, from_x, across, got, noise, from_y, spread, weights, border)
    def paired(edge, start):
        pairs = []
        for i in range(members):
            for j in range(bands):
                k = j + 1 if (j - start) % 2 == 0 else j - 1
                there = (i, k) if min(j, k) >= start and k < bands else (i ^ 1, j)
                pairs.append((i * bands + j, there[0] * bands + there[1]))
        return lax.ppermute(edge, ("member", "lat"), pairs)

    first, second = paired(first, 0), paired(second, 1)
    near, inner, gain_up = pl.pallas_call(
        inner_kernel,
        out_shape=(
            shape(64, width), shape(rows - 4, cols, width), shape(1, w_up.shape[1], dtype=f32)
        ),
        in_specs=[vmem] * 7,
        out_specs=(vmem,) * 3,
        scratch_shapes=[
            pltpu.VMEM(((rows + 4) * 16, width), bf16),
            pltpu.VMEM(((rows - 2) * 16, B * width), bf16),
            pltpu.VMEM(((rows - 4) * cols, B * width), f32),
        ],
        cost_estimate=pl.CostEstimate(
            flops=800_000_000, bytes_accessed=2_000_000, transcendentals=400_000
        ),
        compiler_params=params,
    )(state, weights, *dense)
    result = pl.pallas_call(
        edge_kernel,
        out_shape=shape(rows, cols, width),
        in_specs=[vmem] * 12,
        out_specs=pl.BlockSpec(memory_space=pl.ANY),
        scratch_shapes=[
            pltpu.VMEM(((rows + 4) * 16, width), bf16),
            pltpu.VMEM((4, cols, width), bf16),
            pltpu.SemaphoreType.DMA((3,)),
        ],
        cost_estimate=pl.CostEstimate(
            flops=100_000_000, bytes_accessed=2_000_000, transcendentals=50_000
        ),
        compiler_params=params,
    )(state, near, inner, first, second, weights, *dense, gain_up)
    return result[None]


def solution(mesh):
    circle = mesh.shape["lon"] == 2 and mesh.shape["member"] == 4
    return jax.shard_map(
        circle_shards if circle else window_shards,
        mesh=mesh,
        in_specs=(
            P("lat", "lon", "member"),
            P("member", "lat", "lon", None),
            P(),
            P("lat", None),
            P("lat", None),
            P("lat", None, None),
            P(),
            P(),
            P(),
            P(),
            P(),
        ),
        out_specs=P("member", "lat", "lon", None),
        check_vma=False,
    )
```
